32 devices in a mesh: blk: 8 (over z, y), grp: 4 (over x, core).
Axes of the slice: x: 2, y: 2, z: 4, core: 2. Of those that a mesh axis runs over, the one named last changes fastest.
Arguments:
- view_spectra: bfloat16 [8, 2, 128, 128], P('blk', None, 'grp'), may hold values from -6 to 6
- search_states: int32 [8], P('blk'), may hold values from 0 to 3
- micrograph_spectra: bfloat16 [16, 2, 128, 128], P('blk'), may hold values from -6 to 6
- defocus: float32 [8], replicated, may hold values from 20 to 60
- micrograph_group: int32 [2], replicated, may hold values from 0 to 7
Outputs:
- peak_map: float32 [16, 256, 256], P('blk', 'grp')
- zscore_map: float32 [16, 256, 256], P('blk', 'grp')
The draws below stay inside these ranges and needn't reach their ends.
All inputs are finite; a program needn't handle non-finite values.
Results may differ from the reference program's by a relative error of at most 0.0035.
Values may be sent and summed in bfloat16 or wider, within the bound.
A program may use at most 64 MiB of HBM per device.

```python
import jax
import jax.numpy as jnp
from jax import lax

BOX = 256
KF = 128
MICROGRAPHS = 2
GROUPS = 8
TILES = 16
NV = 8


def set_ends(values, own_key, low, top_value):
    longest = values.shape.index(max(values.shape))
    spots = []
    for shift in (0, 1):
        where = [jax.random.randint(jax.random.fold_in(own_key, axis), (), 0, length) for axis, length in enumerate(values.shape)]
        where[longest] = (where[longest] + shift) % values.shape[longest]
        spots.append(tuple(where))
    return values.at[spots[0]].set(low).at[spots[1]].set(top_value)


def levels(rng, dims, pieces, least, top_value):
    def one(dim, blocks):
        steps = jax.random.uniform(jax.random.fold_in(jax.random.fold_in(rng, 6), dim), (blocks,), jnp.float32, least / len(pieces), top_value / len(pieces))
        return jnp.repeat(jnp.exp(steps), dims[dim] // blocks).reshape((-1,) + (1,) * (len(dims) - dim - 1))

    factor_of = one(*pieces[0])
    for cut in pieces[1:]:
        factor_of = factor_of * one(*cut)
    return factor_of


def normal_values(stream_key, extent, scale, reach, cuts=(), kind=jnp.bfloat16):
    loudness = levels(stream_key, extent, cuts, -0.22, 0.18) if cuts else 1.0
    values = jax.random.normal(stream_key, extent, jnp.float32) * scale * loudness
    return jnp.minimum(jnp.maximum(values, -reach), reach).astype(kind)


def setup_inputs(seed: int = 0) -> dict:
    splits = jax.random.split(jax.random.key(seed), 6)
    view_spectra = normal_values(splits[0], (NV, 2, KF, KF), 1.0, 6.0, ((0, 8), (2, 4)))
    search_states = set_ends(jax.random.randint(splits[1], (NV,), 0, 4), jax.random.fold_in(splits[1], 1), 0, 3).astype(jnp.int32)
    micrograph_spectra = normal_values(splits[2], (TILES, 2, KF, KF), 1.0, 6.0, ((0, 8),))
    defocus = jnp.clip(jax.random.uniform(splits[3], (GROUPS,), jnp.float32, 20.0, 60.0), 20.0, 60.0)
    micrograph_group = jax.random.randint(splits[4], (MICROGRAPHS,), 0, GROUPS).astype(jnp.int32)
    return dict(view_spectra=view_spectra, search_states=search_states, micrograph_spectra=micrograph_spectra, defocus=defocus, micrograph_group=micrograph_group)


focus_offset = 3.0
phase_shift = 0.1

def dft_tables(count):
    position = jnp.arange(count, dtype=jnp.int32)[:, None]
    frequency = jnp.arange(KF, dtype=jnp.int32)[None, :] - KF // 2
    phase = jnp.mod(position * frequency, BOX).astype(jnp.float32) * (2.0 * jnp.pi / BOX)
    return (jnp.cos(phase).astype(jnp.bfloat16), jnp.sin(phase).astype(jnp.bfloat16))

def radius_grid():
    frequency = (jnp.arange(KF, dtype=jnp.int32) - KF // 2).astype(jnp.float32)
    return (frequency[:, None] ** 2 + frequency[None, :] ** 2) / float(KF * KF)

def reference(view_spectra, search_states, micrograph_spectra, defocus, micrograph_group):
    cos_tab, sin_tab = dft_tables(BOX)
    left_table = jnp.concatenate([jnp.concatenate([cos_tab, -sin_tab], axis=1), jnp.concatenate([sin_tab, cos_tab], axis=1)], axis=0).astype(jnp.float32)
    cos_y = cos_tab.astype(jnp.float32)
    sin_y = sin_tab.astype(jnp.float32)
    radius_sq = radius_grid()
    tile_ids = jnp.arange(TILES, dtype=jnp.int32)
    micro_ids = tile_ids // (TILES // MICROGRAPHS)
    base_focus = defocus[micrograph_group[micro_ids]]
    micro_real = micrograph_spectra[:, 0].astype(jnp.float32)
    micro_imag = micrograph_spectra[:, 1].astype(jnp.float32)

    def score_view(running, scan_input):
        spectrum, variant = scan_input
        flip_sign = 1.0 - 2.0 * jnp.mod(variant, 2).astype(jnp.float32)
        focus_step = (variant // 2).astype(jnp.float32)
        real_part = spectrum[0].astype(jnp.float32)
        imag_part = spectrum[1].astype(jnp.float32) * flip_sign
        defocus_now = base_focus + focus_offset * (2.0 * focus_step - 1.0)
        transfer = -jnp.sin(defocus_now[:, None, None] * radius_sq[None] + phase_shift)
        prod_real = (transfer * (real_part * micro_real + imag_part * micro_imag)).astype(jnp.bfloat16)
        prod_imag = (transfer * (real_part * micro_imag - imag_part * micro_real)).astype(jnp.bfloat16)
        stacked = jnp.concatenate([prod_real, prod_imag], axis=1).astype(jnp.float32)
        section_one = jnp.einsum('ab,tbk->tak', left_table, stacked).astype(jnp.bfloat16).astype(jnp.float32)
        part_a = section_one[:, :BOX]
        part_b = section_one[:, BOX:]
        scores = (jnp.einsum('txk,yk->txy', part_a, cos_y) - jnp.einsum('txk,yk->txy', part_b, sin_y)) / KF
        peak_map, totals, squares = running
        return ((jnp.maximum(peak_map, scores), totals + scores, squares + scores * scores), None)
    shape = (TILES, BOX, BOX)
    start_state = (jnp.full(shape, -1e+30, jnp.float32), jnp.zeros(shape, jnp.float32), jnp.zeros(shape, jnp.float32))
    running, unused = lax.scan(score_view, start_state, (view_spectra, search_states))
    peak_map, totals, squares = running
    mean_map = totals / NV
    variance = squares / NV - mean_map * mean_map
    zscore_map = (peak_map - mean_map) / jnp.sqrt(variance + 1e-05)
    return (peak_map, zscore_map)
```

```python
import functools
import math

import jax
import jax.numpy as jnp
import ml_dtypes
import numpy as np
from jax import lax
from jax.experimental import pallas as pl
from jax.experimental.pallas import tpu as pltpu
from jax.sharding import PartitionSpec as P

BOX = 256
KF = 128
MICROGRAPHS = 2
focus_offset = 3.0
phase_shift = 0.1
MESH = pl.DeviceIdType.MESH
f32, bf16 = jnp.float32, jnp.bfloat16


def dft_tables():
    position = np.arange(BOX)[:, None]
    frequency = np.arange(KF)[None, :] - KF // 2
    phase = np.mod(position * frequency, BOX) * (2.0 * np.pi / BOX)
    return np.cos(phase), np.sin(phase)


def constant_tables(groups):
    cos, sin = dft_tables()
    columns = BOX // groups
    left = []
    for g in range(groups):
        c, s = (tab[g * columns : (g + 1) * columns] for tab in (cos, sin))
        left.append(np.block([[c, -s], [s, c]]))
    right = np.concatenate([cos.T, -sin.T], axis=0) / KF
    return np.stack(left).astype(ml_dtypes.bfloat16), right.astype(ml_dtypes.bfloat16)


def flip_bits(index, mask, size):
    bits = int(math.log2(size))
    return sum(((index // 2**i + mask // 2**i) % 2) * 2**i for i in range(bits))


def kernel(
    n,
    groups,
    tiles,
    views_ref,
    states_ref,
    micro_ref,
    defocus_ref,
    group_ref,
    left_ref,
    right_ref,
    peak_ref,
    zscore_ref,
    spectra,
    flags,
    filtered,
    totals,
    squares,
    blk_send,
    blk_recv,
    flag_send,
    flag_recv,
    x_send,
    x_recv,
    core_send,
    core_recv,
    far_send,
    far_recv,
):
    b, g = lax.axis_index("blk"), lax.axis_index("grp")
    g_core = g + 1 - 2 * (g % 2)
    g_x = (g + 2) % groups
    g_far = (g_core + 2) % groups
    rows = views_ref.shape[2]
    columns = BOX // groups
    unroll = n <= 8

    def each(low, high, body):
        if unroll:
            for d in range(low, high):
                body(d)
        else:
            lax.fori_loop(low, high, lambda d, carry: (body(d), carry)[1], 0)

    def peer(d):
        return flip_bits(b, d, n)

    def to(block, group):
        return dict(device_id=(block, group), device_id_type=MESH)

    def blk_copy(d, source):
        part = spectra.at[source, g]
        return pltpu.make_async_remote_copy(
            part, part, blk_send.at[d], blk_recv.at[d], **to(peer(d), g)
        )

    def flag_copy(d, source):
        part = flags.at[source]
        return pltpu.make_async_remote_copy(
            part, part, flag_send.at[d], flag_recv.at[d], **to(peer(d), g)
        )

    def x_copy(d, group):
        part = spectra.at[peer(d), group]
        return pltpu.make_async_remote_copy(
            part, part, x_send.at[d], x_recv.at[d], **to(b, g_x)
        )

    def core_copy(d, group):
        part = spectra.at[peer(d), group]
        return pltpu.make_async_remote_copy(
            part, part, core_send.at[d], core_recv.at[d], **to(b, g_core)
        )

    def far_copy(d, group):
        part = spectra.at[peer(d), group]
        return pltpu.make_async_remote_copy(
            part, part, far_send.at[d], far_recv.at[d], **to(b, g_core)
        )

    barrier = pltpu.get_barrier_semaphore()
    each(1, n, lambda d: pl.semaphore_signal(barrier, inc=1, **to(peer(d), g)))
    pl.semaphore_signal(barrier, inc=1, **to(b, g_x))
    pl.semaphore_signal(barrier, inc=1, **to(b, g_core))

    state = states_ref[0]
    flip = (1 - 2 * (state % 2)).astype(f32)
    spectra[b, g, 0] = views_ref[0, 0]
    spectra[b, g, 1] = (views_ref[0, 1].astype(f32) * flip).astype(bf16)
    flags[b] = jnp.full((1, KF), (state // 2).astype(f32), f32)
    pl.semaphore_wait(barrier, n + 1)

    x_copy(0, g).start()
    core_copy(0, g).start()

    def send_own(d):
        blk_copy(d, b).start()
        flag_copy(d, b).start()

    each(1, n, send_own)

    micro = (b * tiles) // (n * tiles // MICROGRAPHS)
    base = defocus_ref[group_ref[micro]]
    row_f = (lax.broadcasted_iota(jnp.int32, (KF, KF), 0) - KF // 2).astype(f32)
    col_f = (lax.broadcasted_iota(jnp.int32, (KF, KF), 1) - KF // 2).astype(f32)
    radius_sq = (row_f * row_f + col_f * col_f) * (1.0 / (KF * KF))
    for step in range(2):
        transfer = -jnp.sin((base + focus_offset * (2.0 * step - 1.0)) * radius_sq + phase_shift)
        for t in range(tiles):
            for part in range(2):
                filtered[step, t, part] = transfer * micro_ref[t, part].astype(f32)

    def forward_blk(d):
        blk_copy(d, peer(d)).wait_recv()
        x_copy(d, g).start()
        core_copy(d, g).start()

    def forward_x(d):
        x_copy(d, g_x).wait_recv()
        far_copy(d, g_x).start()

    def score(d, first):
        v = peer(d)
        core_copy(d, g_core).wait_recv()
        far_copy(d, g_far).wait_recv()
        real = spectra[v, :, 0].reshape(KF, KF).astype(f32)
        imag = spectra[v, :, 1].reshape(KF, KF).astype(f32)
        later = jnp.broadcast_to(flags[v], (KF, KF)) > 0.5
        stacks = []
        for t in range(tiles):
            m_real = jnp.where(later, filtered[1, t, 0], filtered[0, t, 0])
            m_imag = jnp.where(later, filtered[1, t, 1], filtered[0, t, 1])
            prod_real = (real * m_real + imag * m_imag).astype(bf16)
            prod_imag = (real * m_imag - imag * m_real).astype(bf16)
            stacks.append(jnp.concatenate([prod_real, prod_imag], axis=0))
        stacked = jnp.concatenate(stacks, axis=1)
        section = jnp.dot(left_ref[g], stacked, preferred_element_type=f32).astype(bf16)
        lines = jnp.concatenate(
            [
                jnp.concatenate(
                    [
                        section[:columns, t * KF : (t + 1) * KF],
                        section[columns:, t * KF : (t + 1) * KF],
                    ],
                    axis=1,
                )
                for t in range(tiles)
            ],
            axis=0,
        )
        scores = jnp.dot(lines, right_ref[...], preferred_element_type=f32)
        scores = scores.reshape(tiles, columns, BOX)
        if first:
            peak_ref[...] = scores
            totals[...] = scores
            squares[...] = scores * scores
        else:
            peak_ref[...] = jnp.maximum(peak_ref[...], scores)
            totals[...] += scores
            squares[...] += scores * scores

    def wait_flag(d):
        flag_copy(d, peer(d)).wait_recv()

    if unroll:
        for d in range(n + 2):
            if 1 <= d < n:
                forward_blk(d)
            if 1 <= d <= n:
                forward_x(d - 1)
            if d >= 2:
                if d > 2:
                    wait_flag(d - 2)
                score(d - 2, d == 2)
    else:
        forward_x(0)

        def pump(d):
            forward_blk(d)
            wait_flag(d)

        each(1, n, pump)
        each(1, n, forward_x)
        score(0, True)
        each(1, n, lambda d: score(d, False))

    total = 1.0 / n
    mean = totals[...] * total
    variance = squares[...] * total - mean * mean
    zscore_ref[...] = (peak_ref[...] - mean) * lax.rsqrt(variance + 1e-5)

    def drain(d):
        x_copy(d, g).wait_send()
        core_copy(d, g).wait_send()
        far_copy(d, g_x).wait_send()

    def drain_own(d):
        blk_copy(d, b).wait_send()
        flag_copy(d, b).wait_send()

    each(0, n, drain)
    each(1, n, drain_own)


def solution(mesh):
    n, groups = mesh.shape["blk"], mesh.shape["grp"]
    left, right = constant_tables(groups)

    def per_device(view_spectra, search_states, micrograph_spectra, defocus, micrograph_group):
        tiles = micrograph_spectra.shape[0]
        rows = view_spectra.shape[2]
        columns = BOX // groups
        vmem = pl.BlockSpec(memory_space=pltpu.VMEM)
        smem = pl.BlockSpec(memory_space=pltpu.SMEM)
        out = jax.ShapeDtypeStruct((tiles, columns, BOX), f32)
        return pl.pallas_call(
            functools.partial(kernel, n, groups, tiles),
            out_shape=(out, out),
            in_specs=[vmem, smem, vmem, smem, smem, vmem, vmem],
            out_specs=(vmem, vmem),
            scratch_shapes=[
                pltpu.VMEM((n, groups, 2, rows, KF), bf16),
                pltpu.VMEM((n, 1, KF), f32),
                pltpu.VMEM((2, tiles, 2, KF, KF), f32),
                pltpu.VMEM((tiles, columns, BOX), f32),
                pltpu.VMEM((tiles, columns, BOX), f32),
            ]
            + [pltpu.SemaphoreType.DMA((n,))] * 10,
            compiler_params=pltpu.CompilerParams(
                collective_id=0, has_side_effects=True, vmem_limit_bytes=32 * 2**20
            ),
        )(
            view_spectra,
            search_states,
            micrograph_spectra,
            defocus,
            micrograph_group,
            jnp.asarray(left),
            jnp.asarray(right),
        )

    return jax.shard_map(
        per_device,
        mesh=mesh,
        in_specs=(P("blk", None, "grp", None), P("blk"), P("blk", None, None, None), P(), P()),
        out_specs=(P("blk", "grp", None), P("blk", "grp", None)),
        check_vma=False,
    )
```

```python
import functools
import math

import jax
import jax.numpy as jnp
import ml_dtypes
import numpy as np
from jax import lax
from jax.experimental import pallas as pl
from jax.experimental.pallas import tpu as pltpu
from jax.sharding import PartitionSpec as P

BOX = 256
KF = 128
MICROGRAPHS = 2
focus_offset = 3.0
phase_shift = 0.1
MESH = pl.DeviceIdType.MESH
f32, bf16 = jnp.float32, jnp.bfloat16


def dft_tables():
    position = np.arange(BOX)[:, None]
    frequency = np.arange(KF)[None, :] - KF // 2
    phase = np.mod(position * frequency, BOX) * (2.0 * np.pi / BOX)
    return np.cos(phase), np.sin(phase)


def constant_tables(groups):
    cos, sin = dft_tables()
    columns = BOX // groups
    left = []
    for g in range(groups):
        c, s = (tab[g * columns : (g + 1) * columns] for tab in (cos, sin))
        left.append(np.block([[c, -s], [s, c]]))
    right = np.concatenate([cos.T, -sin.T], axis=0) / KF
    return np.stack(left).astype(ml_dtypes.bfloat16), right.astype(ml_dtypes.bfloat16)


def flip_bits(bits, mask):
    return sum(lax.rem(bit + lax.rem(lax.div(mask, 2**i), 2), 2) * 2**i for i, bit in enumerate(bits))


def sine(x):
    turns = jnp.round(x * (1.0 / math.pi))
    r = (x - turns * 3.140625) - turns * (math.pi - 3.140625)
    half = turns * 0.5
    sign = 1.0 - 4.0 * jnp.abs(half - jnp.floor(half))
    r2 = r * r
    poly = -2.5052108e-8
    for c in (2.7557319e-6, -1.9841270e-4, 8.3333333e-3, -1.6666667e-1):
        poly = poly * r2 + c
    return sign * (r + r * (r2 * poly))


def kernel(
    n,
    groups,
    tiles,
    views_hbm,
    states_hbm,
    micro_hbm,
    defocus_hbm,
    group_hbm,
    left_hbm,
    right_hbm,
    peak_ref,
    zscore_ref,
    views_ref,
    states_ref,
    micro_ref,
    defocus_ref,
    group_ref,
    left_ref,
    right_ref,
    fetch_sem,
    spectra,
    flags,
    filtered,
    totals,
    squares,
    blk_send,
    blk_recv,
    flag_send,
    flag_recv,
    core_send,
    core_recv,
):
    b, g = lax.axis_index("blk"), lax.axis_index("grp")
    g_core = g + 1 - 2 * (g % 2)
    g_x = (g + 2) % groups
    g_far = (g_core + 2) % groups
    rows = views_ref.shape[2]
    columns = BOX // groups
    unroll = n <= 8

    def each(low, high, body):
        if unroll:
            for d in range(low, high):
                body(d)
        else:
            lax.fori_loop(low, high, lambda d, carry: (body(d), carry)[1], 0)

    bits = [lax.rem(lax.div(b, 2**i), 2) for i in range(int(math.log2(n)))]
    peers = []
    if unroll:
        for d in range(n):
            signs = [(1 - 2 * bit) * 2**i for i, bit in enumerate(bits) if d >> i & 1]
            peers.append(sum(signs, b))

    def peer(d):
        return peers[d] if unroll else flip_bits(bits, d)

    def to(block, group):
        return dict(device_id=(block, group), device_id_type=MESH)

    def direct_copy(d, side, block, group):
        part = spectra.at[block, group]
        i = 2 * d + side
        return pltpu.make_async_remote_copy(
            part, part, blk_send.at[i], blk_recv.at[i], **to(peer(d), g_x if side else g)
        )

    def flag_copy(d, source):
        part = flags.at[source]
        return pltpu.make_async_remote_copy(
            part, part, flag_send.at[d], flag_recv.at[d], **to(peer(d), g)
        )

    def core_copy(d, side, group):
        part = spectra.at[peer(d), group]
        i = 2 * d + side
        return pltpu.make_async_remote_copy(
            part, part, core_send.at[i], core_recv.at[i], **to(b, g_core)
        )

    fetches = [
        pltpu.make_async_copy(source, target, fetch_sem.at[i])
        for i, (source, target) in enumerate(
            [
                (states_hbm, states_ref),
                (views_hbm, views_ref),
                (group_hbm, group_ref),
                (defocus_hbm, defocus_ref),
                (micro_hbm, micro_ref),
                (left_hbm.at[g], left_ref),
                (right_hbm, right_ref),
            ]
        )
    ]
    barrier = pltpu.get_barrier_semaphore()
    each(1, n, lambda d: pl.semaphore_signal(barrier, inc=1, **to(peer(d), g)))
    each(0, n, lambda d: pl.semaphore_signal(barrier, inc=1, **to(peer(d), g_x)))
    pl.semaphore_signal(barrier, inc=1, **to(b, g_core))
    for fetch in fetches:
        fetch.start()
    for fetch in fetches[:2]:
        fetch.wait()

    state = states_ref[0]
    flip = (1 - 2 * (state % 2)).astype(f32)
    spectra[b, g, 0] = views_ref[0, 0]
    spectra[b, g, 1] = (views_ref[0, 1].astype(f32) * flip).astype(bf16)
    flags[b] = jnp.full((1, KF), (state // 2).astype(f32), f32)
    pl.semaphore_wait(barrier, 2 * n)

    def send_own(i):
        d = n - 1 - i
        direct_copy(d, 0, b, g).start()
        direct_copy(d, 1, b, g).start()
        flag_copy(d, b).start()

    core_copy(0, 0, g).start()
    each(0, n - 1, send_own)
    direct_copy(0, 1, b, g).start()

    for fetch in fetches[2:]:
        fetch.wait()
    micro = (b * tiles) // (n * tiles // MICROGRAPHS)
    base = defocus_ref[group_ref[micro]]
    row_f = (lax.broadcasted_iota(jnp.int32, (KF, KF), 0) - KF // 2).astype(f32)
    col_f = (lax.broadcasted_iota(jnp.int32, (KF, KF), 1) - KF // 2).astype(f32)
    radius_sq = (row_f * row_f + col_f * col_f) * (1.0 / (KF * KF))
    for step in range(2):
        transfer = -sine((base + focus_offset * (2.0 * step - 1.0)) * radius_sq + phase_shift)
        for t in range(tiles):
            for part in range(2):
                filtered[step, t, part] = transfer * micro_ref[t, part].astype(f32)

    def forward(d, side):
        group = g_x if side else g
        direct_copy(d, side, peer(d), group).wait_recv()
        core_copy(d, side, group).start()

    def forward_both(d):
        forward(d, 0)
        forward(d, 1)
        wait_flag(d)

    def score(d, first):
        v = peer(d)
        core_copy(d, 0, g_core).wait_recv()
        core_copy(d, 1, g_far).wait_recv()
        real = spectra[v, :, 0].reshape(KF, KF).astype(f32)
        imag = spectra[v, :, 1].reshape(KF, KF).astype(f32)
        later = jnp.broadcast_to(flags[v], (KF, KF)) > 0.5
        stacks = []
        for t in range(tiles):
            m_real = jnp.where(later, filtered[1, t, 0], filtered[0, t, 0])
            m_imag = jnp.where(later, filtered[1, t, 1], filtered[0, t, 1])
            prod_real = (real * m_real + imag * m_imag).astype(bf16)
            prod_imag = (real * m_imag - imag * m_real).astype(bf16)
            stacks.append(jnp.concatenate([prod_real, prod_imag], axis=0))
        stacked = jnp.concatenate(stacks, axis=1)
        section = jnp.dot(left_ref[...], stacked, preferred_element_type=f32).astype(bf16)
        lines = jnp.concatenate(
            [
                jnp.concatenate(
                    [
                        section[:columns, t * KF : (t + 1) * KF],
                        section[columns:, t * KF : (t + 1) * KF],
                    ],
                    axis=1,
                )
                for t in range(tiles)
            ],
            axis=0,
        )
        scores = jnp.dot(lines, right_ref[...], preferred_element_type=f32)
        scores = scores.reshape(tiles, columns, BOX)
        if first:
            peak_ref[...] = scores
            totals[...] = scores
            squares[...] = scores * scores
        else:
            peak_ref[...] = jnp.maximum(peak_ref[...], scores)
            totals[...] += scores
            squares[...] += scores * scores

    def wait_flag(d):
        flag_copy(d, peer(d)).wait_recv()

    forward(0, 1)
    each(1, n, forward_both)
    score(0, True)
    each(1, n, lambda d: score(d, False))

    total = 1.0 / n
    mean = totals[...] * total
    variance = squares[...] * total - mean * mean
    zscore_ref[...] = (peak_ref[...] - mean) * lax.rsqrt(variance + 1e-5)

    def drain(d):
        core_copy(d, 0, g).wait_send()
        core_copy(d, 1, g_x).wait_send()
        direct_copy(d, 1, b, g).wait_send()

    def drain_own(d):
        direct_copy(d, 0, b, g).wait_send()
        flag_copy(d, b).wait_send()

    each(0, n, drain)
    each(1, n, drain_own)


def solution(mesh):
    n, groups = mesh.shape["blk"], mesh.shape["grp"]
    left, right = constant_tables(groups)

    def per_device(view_spectra, search_states, micrograph_spectra, defocus, micrograph_group):
        tiles = micrograph_spectra.shape[0]
        rows = view_spectra.shape[2]
        columns = BOX // groups
        vmem = pl.BlockSpec(memory_space=pltpu.VMEM)
        hbm = pl.BlockSpec(memory_space=pltpu.HBM)
        out = jax.ShapeDtypeStruct((tiles, columns, BOX), f32)
        return pl.pallas_call(
            functools.partial(kernel, n, groups, tiles),
            out_shape=(out, out),
            in_specs=[hbm] * 7,
            out_specs=(vmem, vmem),
            scratch_shapes=[
                pltpu.VMEM(view_spectra.shape, bf16),
                pltpu.SMEM(search_states.shape, jnp.int32),
                pltpu.VMEM(micrograph_spectra.shape, bf16),
                pltpu.SMEM(defocus.shape, f32),
                pltpu.SMEM(micrograph_group.shape, jnp.int32),
                pltpu.VMEM(left.shape[1:], bf16),
                pltpu.VMEM(right.shape, bf16),
                pltpu.SemaphoreType.DMA((7,)),
                pltpu.VMEM((n, groups, 2, rows, KF), bf16),
                pltpu.VMEM((n, 1, KF), f32),
                pltpu.VMEM((2, tiles, 2, KF, KF), f32),
                pltpu.VMEM((tiles, columns, BOX), f32),
                pltpu.VMEM((tiles, columns, BOX), f32),
            ]
            + [pltpu.SemaphoreType.DMA((2 * n,))] * 6,
            compiler_params=pltpu.CompilerParams(
                collective_id=0, has_side_effects=True, vmem_limit_bytes=60 * 2**20
            ),
        )(
            view_spectra,
            search_states,
            micrograph_spectra,
            defocus,
            micrograph_group,
            jnp.asarray(left),
            jnp.asarray(right),
        )

    return jax.shard_map(
        per_device,
        mesh=mesh,
        in_specs=(P("blk", None, "grp", None), P("blk"), P("blk", None, None, None), P(), P()),
        out_specs=(P("blk", "grp", None), P("blk", "grp", None)),
        check_vma=False,
    )
```

```python
import functools
import math

import jax
import jax.numpy as jnp
import ml_dtypes
import numpy as np
from jax import lax
from jax.experimental import pallas as pl
from jax.experimental.pallas import tpu as pltpu
from jax.sharding import PartitionSpec as P

BOX = 256
KF = 128
MICROGRAPHS = 2
focus_offset = 3.0
phase_shift = 0.1
MESH = pl.DeviceIdType.MESH
f32, bf16 = jnp.float32, jnp.bfloat16


def dft_tables():
    position = np.arange(BOX)[:, None]
    frequency = np.arange(KF)[None, :] - KF // 2
    phase = np.mod(position * frequency, BOX) * (2.0 * np.pi / BOX)
    return np.cos(phase), np.sin(phase)


def constant_tables(groups):
    cos, sin = dft_tables()
    columns = BOX // groups
    left = []
    for g in range(groups):
        c, s = (tab[g * columns : (g + 1) * columns] for tab in (cos, sin))
        left.append(np.block([[c, -s], [s, c]]))
    right = np.concatenate([cos.T, -sin.T], axis=0) / KF
    return np.stack(left).astype(ml_dtypes.bfloat16), right.astype(ml_dtypes.bfloat16)


def flip_bits(bits, mask):
    return sum(lax.rem(bit + lax.rem(lax.div(mask, 2**i), 2), 2) * 2**i for i, bit in enumerate(bits))


def sine(x):
    turns = jnp.round(x * (1.0 / math.pi))
    r = (x - turns * 3.140625) - turns * (math.pi - 3.140625)
    half = turns * 0.5
    sign = 1.0 - 4.0 * jnp.abs(half - jnp.floor(half))
    r2 = r * r
    poly = -2.5052108e-8
    for c in (2.7557319e-6, -1.9841270e-4, 8.3333333e-3, -1.6666667e-1):
        poly = poly * r2 + c
    return sign * (r + r * (r2 * poly))


def kernel(
    n,
    groups,
    tiles,
    states_ref,
    views_hbm,
    micro_hbm,
    defocus_hbm,
    group_hbm,
    left_hbm,
    right_hbm,
    peak_ref,
    totals,
    squares,
    views_ref,
    micro_ref,
    defocus_ref,
    group_ref,
    left_ref,
    right_ref,
    fetch_sem,
    spectra,
    flags,
    filtered,
    blk_send,
    blk_recv,
    flag_send,
    flag_recv,
    core_send,
    core_recv,
):
    b, g = lax.axis_index("blk"), lax.axis_index("grp")
    g_core = g + 1 - 2 * (g % 2)
    g_x = (g + 2) % groups
    g_far = (g_core + 2) % groups
    rows = views_ref.shape[2]
    columns = BOX // groups
    unroll = n <= 8

    def each(low, high, body):
        if unroll:
            for d in range(low, high):
                body(d)
        else:
            lax.fori_loop(low, high, lambda d, carry: (body(d), carry)[1], 0)

    bits = [lax.rem(lax.div(b, 2**i), 2) for i in range(int(math.log2(n)))]
    peers = []
    if unroll:
        for d in range(n):
            signs = [(1 - 2 * bit) * 2**i for i, bit in enumerate(bits) if d >> i & 1]
            peers.append(sum(signs, b))

    def peer(d):
        return peers[d] if unroll else flip_bits(bits, d)

    def to(block, group):
        return dict(device_id=(block, group), device_id_type=MESH)

    def direct_copy(d, side, block, group):
        part = spectra.at[block, group]
        i = 2 * d + side
        return pltpu.make_async_remote_copy(
            part, part, blk_send.at[i], blk_recv.at[i], **to(peer(d), g_x if side else g)
        )

    def flag_copy(d, source):
        part = flags.at[source]
        return pltpu.make_async_remote_copy(
            part, part, flag_send.at[d], flag_recv.at[d], **to(peer(d), g)
        )

    def core_copy(d, side, group):
        part = spectra.at[peer(d), group]
        i = 2 * d + side
        return pltpu.make_async_remote_copy(
            part, part, core_send.at[i], core_recv.at[i], **to(b, g_core)
        )

    fetches = [
        pltpu.make_async_copy(source, target, fetch_sem.at[i])
        for i, (source, target) in enumerate(
            [
                (views_hbm, views_ref),
                (group_hbm, group_ref),
                (defocus_hbm, defocus_ref),
                (micro_hbm, micro_ref),
                (left_hbm.at[g], left_ref),
                (right_hbm, right_ref),
            ]
        )
    ]
    barrier = pltpu.get_barrier_semaphore()
    each(1, n, lambda d: pl.semaphore_signal(barrier, inc=1, **to(peer(d), g)))
    each(0, n, lambda d: pl.semaphore_signal(barrier, inc=1, **to(peer(d), g_x)))
    pl.semaphore_signal(barrier, inc=1, **to(b, g_core))
    for fetch in fetches:
        fetch.start()
    for fetch in fetches[:1]:
        fetch.wait()

    state = states_ref[0]
    flip = (1 - 2 * (state % 2)).astype(f32)
    spectra[b, g, 0] = views_ref[0, 0]
    spectra[b, g, 1] = (views_ref[0, 1].astype(f32) * flip).astype(bf16)
    flags[b] = jnp.full((1, KF), (state // 2).astype(f32), f32)
    pl.semaphore_wait(barrier, 2 * n)

    def send_own(i):
        d = n - 1 - i
        direct_copy(d, 0, b, g).start()
        direct_copy(d, 1, b, g).start()
        flag_copy(d, b).start()

    core_copy(0, 0, g).start()
    each(0, n - 1, send_own)
    direct_copy(0, 1, b, g).start()

    for fetch in fetches[1:]:
        fetch.wait()
    micro = (b * tiles) // (n * tiles // MICROGRAPHS)
    base = defocus_ref[group_ref[micro]]
    row_f = (lax.broadcasted_iota(jnp.int32, (KF, KF), 0) - KF // 2).astype(f32)
    col_f = (lax.broadcasted_iota(jnp.int32, (KF, KF), 1) - KF // 2).astype(f32)
    radius_sq = (row_f * row_f + col_f * col_f) * (1.0 / (KF * KF))
    for step in range(2):
        transfer = -sine((base + focus_offset * (2.0 * step - 1.0)) * radius_sq + phase_shift)
        for t in range(tiles):
            for part in range(2):
                filtered[step, t, part] = transfer * micro_ref[t, part].astype(f32)

    def forward(d, side):
        group = g_x if side else g
        direct_copy(d, side, peer(d), group).wait_recv()
        core_copy(d, side, group).start()

    def forward_both(d):
        forward(d, 0)
        forward(d, 1)
        wait_flag(d)

    def score(d, first):
        v = peer(d)
        core_copy(d, 0, g_core).wait_recv()
        core_copy(d, 1, g_far).wait_recv()
        real = spectra[v, :, 0].reshape(KF, KF).astype(f32)
        imag = spectra[v, :, 1].reshape(KF, KF).astype(f32)
        later = jnp.broadcast_to(flags[v], (KF, KF)) > 0.5
        stacks = []
        for t in range(tiles):
            m_real = jnp.where(later, filtered[1, t, 0], filtered[0, t, 0])
            m_imag = jnp.where(later, filtered[1, t, 1], filtered[0, t, 1])
            prod_real = (real * m_real + imag * m_imag).astype(bf16)
            prod_imag = (real * m_imag - imag * m_real).astype(bf16)
            stacks.append(jnp.concatenate([prod_real, prod_imag], axis=0))
        stacked = jnp.concatenate(stacks, axis=1)
        section = jnp.dot(left_ref[...], stacked, preferred_element_type=f32).astype(bf16)
        lines = jnp.concatenate(
            [
                jnp.concatenate(
                    [
                        section[:columns, t * KF : (t + 1) * KF],
                        section[columns:, t * KF : (t + 1) * KF],
                    ],
                    axis=1,
                )
                for t in range(tiles)
            ],
            axis=0,
        )
        scores = jnp.dot(lines, right_ref[...], preferred_element_type=f32)
        scores = scores.reshape(tiles, columns, BOX)
        if first:
            peak_ref[...] = scores
            totals[...] = scores
            squares[...] = scores * scores
        else:
            peak_ref[...] = jnp.maximum(peak_ref[...], scores)
            totals[...] += scores
            squares[...] += scores * scores

    def wait_flag(d):
        flag_copy(d, peer(d)).wait_recv()

    forward(0, 1)
    each(1, n, forward_both)
    score(0, True)
    each(1, n, lambda d: score(d, False))

    def drain(d):
        core_copy(d, 0, g).wait_send()
        core_copy(d, 1, g_x).wait_send()
        direct_copy(d, 1, b, g).wait_send()

    def drain_own(d):
        direct_copy(d, 0, b, g).wait_send()
        flag_copy(d, b).wait_send()

    each(0, n, drain)
    each(1, n, drain_own)


def finish(n, best_ref, totals_ref, squares_ref, peak_ref, zscore_ref):
    mean = totals_ref[...] * (1.0 / n)
    variance = squares_ref[...] * (1.0 / n) - mean * mean
    peak_ref[...] = best_ref[...]
    zscore_ref[...] = (best_ref[...] - mean) * lax.rsqrt(variance + 1e-5)


def solution(mesh):
    n, groups = mesh.shape["blk"], mesh.shape["grp"]
    left, right = constant_tables(groups)

    def per_device(view_spectra, search_states, micrograph_spectra, defocus, micrograph_group):
        tiles = micrograph_spectra.shape[0]
        rows = view_spectra.shape[2]
        columns = BOX // groups
        vmem = pl.BlockSpec(memory_space=pltpu.VMEM)
        hbm = pl.BlockSpec(memory_space=pltpu.HBM)
        out = jax.ShapeDtypeStruct((tiles, columns, BOX), f32)
        sums = pl.pallas_call(
            functools.partial(kernel, n, groups, tiles),
            out_shape=(pltpu.VMEM(out.shape, f32),) * 3,
            in_specs=[pl.BlockSpec(memory_space=pltpu.SMEM)] + [hbm] * 6,
            out_specs=(vmem,) * 3,
            scratch_shapes=[
                pltpu.VMEM(view_spectra.shape, bf16),
                pltpu.VMEM(micrograph_spectra.shape, bf16),
                pltpu.SMEM(defocus.shape, f32),
                pltpu.SMEM(micrograph_group.shape, jnp.int32),
                pltpu.VMEM(left.shape[1:], bf16),
                pltpu.VMEM(right.shape, bf16),
                pltpu.SemaphoreType.DMA((6,)),
                pltpu.VMEM((n, groups, 2, rows, KF), bf16),
                pltpu.VMEM((n, 1, KF), f32),
                pltpu.VMEM((2, tiles, 2, KF, KF), f32),
            ]
            + [pltpu.SemaphoreType.DMA((2 * n,))] * 6,
            compiler_params=pltpu.CompilerParams(
                collective_id=0, has_side_effects=True, vmem_limit_bytes=24 * 2**20
            ),
        )(
            search_states,
            *(
                pltpu.with_memory_space_constraint(x, pltpu.HBM)
                for x in (
                    view_spectra,
                    micrograph_spectra,
                    defocus,
                    micrograph_group,
                    jnp.asarray(left),
                    jnp.asarray(right),
                )
            )
        )
        return pl.pallas_call(
            functools.partial(finish, n),
            out_shape=(out, out),
            in_specs=[vmem] * 3,
            out_specs=(vmem, vmem),
        )(*(pltpu.with_memory_space_constraint(x, pltpu.VMEM) for x in sums))

    return jax.shard_map(
        per_device,
        mesh=mesh,
        in_specs=(P("blk", None, "grp", None), P("blk"), P("blk", None, None, None), P(), P()),
        out_specs=(P("blk", "grp", None), P("blk", "grp", None)),
        check_vma=False,
    )
```

```python
import functools
import math

import jax
import jax.numpy as jnp
import ml_dtypes
import numpy as np
from jax import lax
from jax.experimental import pallas as pl
from jax.experimental.pallas import tpu as pltpu
from jax.sharding import PartitionSpec as P

BOX = 256
KF = 128
MICROGRAPHS = 2
focus_offset = 3.0
phase_shift = 0.1
MESH = pl.DeviceIdType.MESH
f32, bf16 = jnp.float32, jnp.bfloat16


def dft_tables():
    position = np.arange(BOX)[:, None]
    frequency = np.arange(KF)[None, :] - KF // 2
    phase = np.mod(position * frequency, BOX) * (2.0 * np.pi / BOX)
    return np.cos(phase), np.sin(phase)


def constant_tables(groups):
    cos, sin = dft_tables()
    columns = BOX // groups
    left = []
    for g in range(groups):
        c, s = (tab[g * columns : (g + 1) * columns] for tab in (cos, sin))
        left.append(np.block([[c, -s], [s, c]]))
    right = np.concatenate([cos.T, -sin.T], axis=0) / KF
    return np.stack(left).astype(ml_dtypes.bfloat16), right.astype(ml_dtypes.bfloat16)


def flip_bits(bits, mask):
    return sum(lax.rem(bit + lax.rem(lax.div(mask, 2**i), 2), 2) * 2**i for i, bit in enumerate(bits))


def sine(x):
    turns = jnp.round(x * (1.0 / math.pi))
    r = (x - turns * 3.140625) - turns * (math.pi - 3.140625)
    half = turns * 0.5
    sign = 1.0 - 4.0 * jnp.abs(half - jnp.floor(half))
    r2 = r * r
    poly = -2.5052108e-8
    for c in (2.7557319e-6, -1.9841270e-4, 8.3333333e-3, -1.6666667e-1):
        poly = poly * r2 + c
    return sign * (r + r * (r2 * poly))


def kernel(
    n,
    groups,
    tiles,
    states_ref,
    views_hbm,
    micro_hbm,
    defocus_hbm,
    group_hbm,
    left_hbm,
    right_hbm,
    peak_ref,
    totals,
    squares,
    views_ref,
    micro_ref,
    defocus_ref,
    group_ref,
    left_ref,
    right_ref,
    fetch_sem,
    spectra,
    flags,
    filtered,
    blk_send,
    blk_recv,
    flag_send,
    flag_recv,
    core_send,
    core_recv,
):
    b, g = lax.axis_index("blk"), lax.axis_index("grp")
    g_core = g + 1 - 2 * (g % 2)
    g_x = (g + 2) % groups
    g_far = (g_core + 2) % groups
    rows = views_ref.shape[2]
    columns = BOX // groups
    unroll = n <= 8

    def each(low, high, body):
        if unroll:
            for d in range(low, high):
                body(d)
        else:
            lax.fori_loop(low, high, lambda d, carry: (body(d), carry)[1], 0)

    bits = [lax.rem(lax.div(b, 2**i), 2) for i in range(int(math.log2(n)))]
    peers = []
    if unroll:
        for d in range(n):
            signs = [(1 - 2 * bit) * 2**i for i, bit in enumerate(bits) if d >> i & 1]
            peers.append(sum(signs, b))

    def peer(d):
        return peers[d] if unroll else flip_bits(bits, d)

    def to(block, group):
        return dict(device_id=(block, group), device_id_type=MESH)

    def direct_copy(d, side, block, group):
        part = spectra.at[block, group]
        i = 2 * d + side
        return pltpu.make_async_remote_copy(
            part, part, blk_send.at[i], blk_recv.at[i], **to(peer(d), g_x if side else g)
        )

    def flag_copy(d, source):
        part = flags.at[source]
        return pltpu.make_async_remote_copy(
            part, part, flag_send.at[d], flag_recv.at[d], **to(peer(d), g)
        )

    def core_copy(d, side, group):
        part = spectra.at[peer(d), group]
        i = 2 * d + side
        return pltpu.make_async_remote_copy(
            part, part, core_send.at[i], core_recv.at[i], **to(b, g_core)
        )

    fetches = [
        pltpu.make_async_copy(source, target, fetch_sem.at[i])
        for i, (source, target) in enumerate(
            [
                (views_hbm, views_ref),
                (group_hbm, group_ref),
                (defocus_hbm, defocus_ref),
                (micro_hbm, micro_ref),
                (left_hbm.at[g], left_ref),
                (right_hbm, right_ref),
            ]
        )
    ]
    barrier = pltpu.get_barrier_semaphore()
    each(1, n, lambda d: pl.semaphore_signal(barrier, inc=1, **to(peer(d), g)))
    each(0, n, lambda d: pl.semaphore_signal(barrier, inc=1, **to(peer(d), g_x)))
    pl.semaphore_signal(barrier, inc=1, **to(b, g_core))
    for fetch in fetches:
        fetch.start()
    for fetch in fetches[:1]:
        fetch.wait()

    state = states_ref[0]
    flip = (1 - 2 * (state % 2)).astype(f32)
    spectra[b, g, 0] = views_ref[0, 0]
    spectra[b, g, 1] = (views_ref[0, 1].astype(f32) * flip).astype(bf16)
    flags[b] = jnp.full((1, KF), (state // 2).astype(f32), f32)
    pl.semaphore_wait(barrier, 2 * n)

    def send_own(i):
        d = i + 1
        direct_copy(d, 0, b, g).start()
        direct_copy(d, 1, b, g).start()
        flag_copy(d, b).start()

    direct_copy(0, 1, b, g).start()
    core_copy(0, 0, g).start()
    each(0, n - 1, send_own)

    for fetch in fetches[1:]:
        fetch.wait()
    micro = (b * tiles) // (n * tiles // MICROGRAPHS)
    base = defocus_ref[group_ref[micro]]
    row_f = (lax.broadcasted_iota(jnp.int32, (KF, KF), 0) - KF // 2).astype(f32)
    col_f = (lax.broadcasted_iota(jnp.int32, (KF, KF), 1) - KF // 2).astype(f32)
    radius_sq = (row_f * row_f + col_f * col_f) * (1.0 / (KF * KF))
    for step in range(2):
        transfer = -sine((base + focus_offset * (2.0 * step - 1.0)) * radius_sq + phase_shift)
        for t in range(tiles):
            for part in range(2):
                filtered[step, t, part] = transfer * micro_ref[t, part].astype(f32)

    def forward(d, side):
        group = g_x if side else g
        direct_copy(d, side, peer(d), group).wait_recv()
        core_copy(d, side, group).start()

    def forward_both(d):
        forward(d, 0)
        forward(d, 1)
        wait_flag(d)

    def score(d, first):
        v = peer(d)
        core_copy(d, 0, g_core).wait_recv()
        core_copy(d, 1, g_far).wait_recv()
        real = spectra[v, :, 0].reshape(KF, KF).astype(f32)
        imag = spectra[v, :, 1].reshape(KF, KF).astype(f32)
        later = jnp.broadcast_to(flags[v], (KF, KF)) > 0.5
        stacks = []
        for t in range(tiles):
            m_real = jnp.where(later, filtered[1, t, 0], filtered[0, t, 0])
            m_imag = jnp.where(later, filtered[1, t, 1], filtered[0, t, 1])
            prod_real = (real * m_real + imag * m_imag).astype(bf16)
            prod_imag = (real * m_imag - imag * m_real).astype(bf16)
            stacks.append(jnp.concatenate([prod_real, prod_imag], axis=0))
        stacked = jnp.concatenate(stacks, axis=1)
        section = jnp.dot(left_ref[...], stacked, preferred_element_type=f32).astype(bf16)
        lines = jnp.concatenate(
            [
                jnp.concatenate(
                    [
                        section[:columns, t * KF : (t + 1) * KF],
                        section[columns:, t * KF : (t + 1) * KF],
                    ],
                    axis=1,
                )
                for t in range(tiles)
            ],
            axis=0,
        )
        scores = jnp.dot(lines, right_ref[...], preferred_element_type=f32)
        scores = scores.reshape(tiles, columns, BOX)
        if first:
            peak_ref[...] = scores
            totals[...] = scores
            squares[...] = scores * scores
        else:
            peak_ref[...] = jnp.maximum(peak_ref[...], scores)
            totals[...] += scores
            squares[...] += scores * scores

    def wait_flag(d):
        flag_copy(d, peer(d)).wait_recv()

    forward(0, 1)
    if unroll:
        for d in range(1, n + 2):
            if d < n:
                forward_both(d)
            if d >= 2:
                score(d - 2, d == 2)
    else:
        each(1, n, forward_both)
        score(0, True)
        each(1, n, lambda d: score(d, False))

    def drain(d):
        core_copy(d, 0, g).wait_send()
        core_copy(d, 1, g_x).wait_send()
        direct_copy(d, 1, b, g).wait_send()

    def drain_own(d):
        direct_copy(d, 0, b, g).wait_send()
        flag_copy(d, b).wait_send()

    each(0, n, drain)
    each(1, n, drain_own)


def finish(n, best_ref, totals_ref, squares_ref, peak_ref, zscore_ref):
    mean = totals_ref[...] * (1.0 / n)
    variance = squares_ref[...] * (1.0 / n) - mean * mean
    peak_ref[...] = best_ref[...]
    zscore_ref[...] = (best_ref[...] - mean) * lax.rsqrt(variance + 1e-5)


def solution(mesh):
    n, groups = mesh.shape["blk"], mesh.shape["grp"]
    left, right = constant_tables(groups)

    def per_device(view_spectra, search_states, micrograph_spectra, defocus, micrograph_group):
        tiles = micrograph_spectra.shape[0]
        rows = view_spectra.shape[2]
        columns = BOX // groups
        vmem = pl.BlockSpec(memory_space=pltpu.VMEM)
        hbm = pl.BlockSpec(memory_space=pltpu.HBM)
        out = jax.ShapeDtypeStruct((tiles, columns, BOX), f32)
        sums = pl.pallas_call(
            functools.partial(kernel, n, groups, tiles),
            out_shape=(pltpu.VMEM(out.shape, f32),) * 3,
            in_specs=[pl.BlockSpec(memory_space=pltpu.SMEM)] + [hbm] * 6,
            out_specs=(vmem,) * 3,
            scratch_shapes=[
                pltpu.VMEM(view_spectra.shape, bf16),
                pltpu.VMEM(micrograph_spectra.shape, bf16),
                pltpu.SMEM(defocus.shape, f32),
                pltpu.SMEM(micrograph_group.shape, jnp.int32),
                pltpu.VMEM(left.shape[1:], bf16),
                pltpu.VMEM(right.shape, bf16),
                pltpu.SemaphoreType.DMA((6,)),
                pltpu.VMEM((n, groups, 2, rows, KF), bf16),
                pltpu.VMEM((n, 1, KF), f32),
                pltpu.VMEM((2, tiles, 2, KF, KF), f32),
            ]
            + [pltpu.SemaphoreType.DMA((2 * n,))] * 6,
            compiler_params=pltpu.CompilerParams(
                collective_id=0, has_side_effects=True, vmem_limit_bytes=24 * 2**20
            ),
        )(
            search_states,
            *(
                pltpu.with_memory_space_constraint(x, pltpu.HBM)
                for x in (
                    view_spectra,
                    micrograph_spectra,
                    defocus,
                    micrograph_group,
                    jnp.asarray(left),
                    jnp.asarray(right),
                )
            )
        )
        return pl.pallas_call(
            functools.partial(finish, n),
            out_shape=(out, out),
            in_specs=[vmem] * 3,
            out_specs=(vmem, vmem),
        )(*(pltpu.with_memory_space_constraint(x, pltpu.VMEM) for x in sums))

    return jax.shard_map(
        per_device,
        mesh=mesh,
        in_specs=(P("blk", None, "grp", None), P("blk"), P("blk", None, None, None), P(), P()),
        out_specs=(P("blk", "grp", None), P("blk", "grp", None)),
        check_vma=False,
    )
```
